32 devices in a mesh: fsdp: 16 (over z, x, core), rep: 2 (over y).
Axes of the slice: x: 2, y: 2, z: 4, core: 2. Of those that a mesh axis runs over, the one named last changes fastest.
Arguments:
- tokens: bfloat16 [49152, 768], P(('fsdp', 'rep')), may hold values from -6 to 6
- segments: int32 [192, 256], P(('fsdp', 'rep')), may hold values from 0 to 3, never falling along the last dimension, each value on 1 to 128 neighbouring positions
- cotangent: bfloat16 [49152, 768], P(('fsdp', 'rep')), may hold values from -6 to 6
- attn_gain: bfloat16 [768], P(('fsdp', 'rep')), may hold values from 0.25 to 1.75
- attn_shift: bfloat16 [768], P(('fsdp', 'rep')), may hold values from -3 to 3
- qkv_weight: bfloat16 [768, 2304], P(('fsdp', 'rep')), may hold values from -0.21875 to 0.21875
- query_bias: bfloat16 [768], P(('fsdp', 'rep')), may hold values from -3 to 3
- value_bias: bfloat16 [768], P(('fsdp', 'rep')), may hold values from -3 to 3
- out_weight: bfloat16 [768, 768], P(('fsdp', 'rep')), may hold values from -1.25 to 1.25
- out_bias: bfloat16 [768], P(('fsdp', 'rep')), may hold values from -3 to 3
- mlp_gain: bfloat16 [768], P(('fsdp', 'rep')), may hold values from 0.25 to 1.75
- mlp_shift: bfloat16 [768], P(('fsdp', 'rep')), may hold values from -3 to 3
- up_weight: bfloat16 [768, 3072], P(('fsdp', 'rep')), may hold values from -0.21875 to 0.21875
- up_bias: bfloat16 [3072], P(('fsdp', 'rep')), may hold values from -3 to 3
- down_weight: bfloat16 [3072, 768], P(('fsdp', 'rep')), may hold values from -0.15625 to 0.15625
- down_bias: bfloat16 [768], P(('fsdp', 'rep')), may hold values from -3 to 3
Outputs:
- out: bfloat16 [49152, 768], P(('fsdp', 'rep'))
- grad_tokens: float32 [49152, 768], P(('fsdp', 'rep'))
- grad_attn_gain: float32 [768], P(('fsdp', 'rep'))
- grad_attn_shift: float32 [768], P(('fsdp', 'rep'))
- grad_qkv_weight: float32 [768, 2304], P(('fsdp', 'rep'))
- grad_query_bias: float32 [768], P(('fsdp', 'rep'))
- grad_value_bias: float32 [768], P(('fsdp', 'rep'))
- grad_out_weight: float32 [768, 768], P(('fsdp', 'rep'))
- grad_out_bias: float32 [768], P(('fsdp', 'rep'))
- grad_mlp_gain: float32 [768], P(('fsdp', 'rep'))
- grad_mlp_shift: float32 [768], P(('fsdp', 'rep'))
- grad_up_weight: float32 [768, 3072], P(('fsdp', 'rep'))
- grad_up_bias: float32 [3072], P(('fsdp', 'rep'))
- grad_down_weight: float32 [3072, 768], P(('fsdp', 'rep'))
- grad_down_bias: float32 [768], P(('fsdp', 'rep'))
The draws below stay inside these ranges and needn't reach their ends.
Inputs may be any that keep to these rules, and one draw needn't show every extreme that they name: `segments`: within each sequence the numbers never fall; each of the 4 documents has 1 to 128 tokens, one exactly 128.
All inputs are finite; a program needn't handle non-finite values.
Results may differ from the reference program's by a relative error of at most 0.011.
Values may be sent and summed in bfloat16 or wider, within the bound.
A program may use at most 192 MiB of HBM per device.

```python
import math
import jax
import jax.numpy as jnp
import numpy as np
from jax import lax

D = 768
HEADS = 12
FF = 3072
LEN = 256
DOCS = 4
SEQS = 192
TOKENS = 49152


def raised(array, rng, source, target, blocks, factor):
    def block_of(dim):
        return (jnp.arange(array.shape[dim]) // (array.shape[dim] // blocks)).reshape((-1,) + (1,) * (array.ndim - 1 - dim))

    one_side = jax.random.permutation(rng, blocks)[block_of(target)]
    other_side = (block_of(target) + blocks // 2) % blocks
    return jnp.where((block_of(source) == one_side) | (block_of(source) == other_side), factor * array, array)


def level_of(key, extent, split, least, high):
    level = 1.0
    for axis_at, shards_of in split:
        draws = jax.random.uniform(jax.random.fold_in(jax.random.fold_in(key, 6), axis_at), (shards_of,), jnp.float32, least / len(split), high / len(split))
        level = level * jnp.repeat(jnp.exp(draws), extent[axis_at] // shards_of).reshape((-1,) + (1,) * (len(extent) - 1 - axis_at))
    return level


def length_profile(number_of, total, reach, lean):
    weights = [(1 << 20) // math.isqrt(grade ** lean) + 1 for grade in range(2, number_of + 1)]
    surplus, counts = total - reach - (number_of - 1), [1] * (number_of - 1)
    while surplus > 0:
        movable = [i for i in range(number_of - 1) if counts[i] < reach]
        mass, budget = sum([weights[i] for i in movable]), surplus
        for i in movable:
            addition = min(reach - counts[i], max(1, budget * weights[i] // mass), surplus)
            counts[i] = counts[i] + addition
            surplus = surplus - addition
    return np.array([reach] + counts)


def ragged(stream_key, number_of, total, bound, skew):
    if number_of == 2:
        one = jax.random.randint(stream_key, (), max(1, total - bound), min(bound, total - 1) + 1)
        return jnp.stack([one, total - one])
    tallies = jnp.asarray(length_profile(number_of, total, bound, skew), jnp.int32)
    twos = (number_of - 1) // 2
    giver, taker = tallies[1:1 + 2 * twos:2], tallies[2:2 + 2 * twos:2]
    slack = jnp.minimum(giver - 1, bound - taker)
    passed = jax.random.randint(jax.random.fold_in(stream_key, 1), (twos,), 0, 1 << 20) % (slack + 1)
    tallies = tallies.at[1:1 + 2 * twos:2].set(giver - passed).at[2:2 + 2 * twos:2].set(taker + passed)
    return tallies[jax.random.permutation(jax.random.fold_in(stream_key, 2), number_of)]


def bell_draw(key, shape, scale, limit, split=(), held_as=jnp.bfloat16):
    values = jax.random.normal(key, shape, jnp.float32) * scale
    if len(split) > 0:
        values = level_of(key, shape, split, -0.22, 0.18) * values
    return jnp.clip(values, min=-limit, max=limit).astype(held_as)


def bell_draw_with(rng, extent, deviation, reach, pieces, heavy, kind=jnp.bfloat16):
    values = deviation * jax.random.normal(rng, extent, jnp.float32)
    if pieces:
        values = values * level_of(rng, extent, pieces, -0.22, 0.18)
    return jnp.clip(raised(values, jax.random.fold_in(rng, 3), *heavy), -reach, reach).astype(kind)


def setup_inputs(seed: int = 0) -> dict:
    key_of = jax.random.split(jax.random.key(seed), 17)
    tokens = bell_draw_with(key_of[0], (TOKENS, D), 1.0, 6.0, ((0, 32),), (0, 1, 32, 2.75))
    segments = jax.vmap(lambda own: jnp.searchsorted(jnp.cumsum(ragged(own, DOCS, LEN, LEN // 2, 0)), jnp.arange(LEN), side="right"))(jax.random.split(key_of[1], SEQS)).reshape((SEQS, LEN)).astype(jnp.int32)
    cotangent = bell_draw_with(key_of[2], (TOKENS, D), 1.0, 6.0, ((0, 32),), (0, 1, 32, 2.75))
    attn_gain = jnp.clip(1.0 + 0.15 * jax.random.normal(key_of[3], (D,), jnp.float32), 0.25, 1.75).astype(jnp.bfloat16)
    attn_shift = bell_draw(key_of[4], (D,), 0.5, 3.0, ((0, 32),))
    qkv_weight = bell_draw(key_of[5], (D, 3 * D), D ** -0.5, 0.21875, ((0, 32),))
    query_bias = bell_draw(key_of[6], (D,), 0.5, 3.0, ((0, 32),))
    value_bias = bell_draw(key_of[7], (D,), 0.5, 3.0, ((0, 32),))
    out_weight = bell_draw(key_of[8], (D, D), (D // 32) ** -0.5, 1.25, ((0, 32),))
    out_bias = bell_draw(key_of[9], (D,), 0.5, 3.0, ((0, 32),))
    mlp_gain = jnp.clip(1.0 + 0.15 * jax.random.normal(key_of[10], (D,), jnp.float32), 0.25, 1.75).astype(jnp.bfloat16)
    mlp_shift = bell_draw(key_of[11], (D,), 0.5, 3.0, ((0, 32),))
    up_weight = bell_draw(key_of[12], (D, FF), D ** -0.5, 0.21875, ((0, 32),))
    up_bias = bell_draw(key_of[13], (FF,), 0.5, 3.0, ((0, 32),))
    down_weight = bell_draw(key_of[14], (FF, D), (FF // 2) ** -0.5, 0.15625, ((0, 32),))
    down_bias = bell_draw(key_of[15], (D,), 0.5, 3.0, ((0, 32),))
    return dict(tokens=tokens, segments=segments, cotangent=cotangent, attn_gain=attn_gain, attn_shift=attn_shift, qkv_weight=qkv_weight, query_bias=query_bias, value_bias=value_bias, out_weight=out_weight, out_bias=out_bias, mlp_gain=mlp_gain, mlp_shift=mlp_shift, up_weight=up_weight, up_bias=up_bias, down_weight=down_weight, down_bias=down_bias)


@jax.custom_vjp
def low(v):
    return lax.optimization_barrier(v.astype(jnp.bfloat16)).astype(jnp.float32)

@jax.custom_vjp
def low_back(v):
    return v

def low_keep(v):
    return (low(v), None)

def low_pass(kept, grad):
    return (grad,)

def back_keep(v):
    return (v, None)

def back_low(kept, grad):
    return (low(grad),)
low.defvjp(low_keep, low_pass)
low_back.defvjp(back_keep, back_low)
EPSILON = 1e-05
HIGHEST = lax.Precision.HIGHEST

def norm_rows(values, gain, shift):
    center = values - lax.optimization_barrier(jnp.mean(values, axis=-1, keepdims=True))
    spread = lax.optimization_barrier(jnp.mean(center * center, axis=-1, keepdims=True))
    return center * lax.rsqrt(spread + EPSILON) * gain + shift

def gelu_tanh(values):
    return 0.5 * values * (1.0 + jnp.tanh(0.7978845608028654 * (values + 0.044715 * values * values * values)))

def matmul(left, right):
    return jnp.dot(left, right, precision=HIGHEST, preferred_element_type=jnp.float32)

def forward(rows_in, seg_block, params):
    gain_attn, shift_attn, mat_qkv, bias_query, bias_value, mat_out, bias_out, gain_mlp, shift_mlp, mat_up, bias_up, mat_down, bias_down = params
    row_count = rows_in.shape[0]
    seq_count = row_count // LEN
    head_dim = D // HEADS
    normed = low(norm_rows(rows_in, gain_attn, shift_attn))
    qkv_bias = jnp.concatenate([bias_query, jnp.zeros_like(bias_query), bias_value])
    qkv = low_back(low(matmul(normed, mat_qkv) + qkv_bias))
    view = qkv.reshape(seq_count, LEN, 3, HEADS, head_dim)
    queries = view[:, :, 0]
    key_rows = view[:, :, 1]
    value_rows = view[:, :, 2]
    raw = jnp.einsum('sqhd,skhd->shqk', queries, key_rows, precision=HIGHEST)
    scores = low_back(raw * (1.0 / math.sqrt(head_dim)))
    places = jnp.arange(LEN)
    causal = places[None, :] <= places[:, None]
    same_doc = seg_block[:, :, None] == seg_block[:, None, :]
    allowed = jnp.logical_and(same_doc, causal[None])
    masked = jnp.where(allowed[:, None], scores, -1e+30)
    probs = low(jax.nn.softmax(masked, axis=-1))
    mixed = jnp.einsum('shqk,skhd->sqhd', probs, value_rows, precision=HIGHEST).reshape(row_count, D)
    attended = low_back(low(mixed))
    branch = low_back(matmul(attended, mat_out) + bias_out)
    resid = rows_in + branch
    normed_mlp = low(norm_rows(resid, gain_mlp, shift_mlp))
    pre = low_back(matmul(normed_mlp, mat_up) + bias_up)
    hidden = low(gelu_tanh(pre))
    second = low_back(matmul(hidden, mat_down) + bias_down)
    return resid + second

def reference(tokens, segments, cotangent, attn_gain, attn_shift, qkv_weight, query_bias, value_bias, out_weight, out_bias, mlp_gain, mlp_shift, up_weight, up_bias, down_weight, down_bias):
    params = tuple((arr.astype(jnp.float32) for arr in (attn_gain, attn_shift, qkv_weight, query_bias, value_bias, out_weight, out_bias, mlp_gain, mlp_shift, up_weight, up_bias, down_weight, down_bias)))
    per_group = math.gcd(SEQS, max(1, 4096 // LEN))
    groups = SEQS // per_group
    tok_groups = tokens.astype(jnp.float32).reshape(groups, per_group * LEN, D)
    cot_groups = cotangent.astype(jnp.float32).reshape(groups, per_group * LEN, D)
    seg_groups = segments.reshape(groups, per_group, LEN)

    def step(totals, inputs):
        tok_block, seg_block, cot_block = inputs

        def local(rows_in, weights):
            return forward(rows_in, seg_block, weights)
        result, pullback = jax.vjp(local, tok_block, params)
        grad_rows, grad_params = pullback(cot_block)
        totals = jax.tree.map(lambda first, second: first + second, totals, grad_params)
        return (totals, (result.astype(jnp.bfloat16), grad_rows))
    initial = tuple((jnp.zeros_like(arr) for arr in params))
    param_grads, (results, grad_rows) = lax.scan(step, initial, (tok_groups, seg_groups, cot_groups))
    return (results.reshape(TOKENS, D), grad_rows.reshape(TOKENS, D)) + tuple(param_grads)
```

```python
import functools
import math

import jax
import jax.numpy as jnp
from jax import lax
from jax.experimental import pallas as pl
from jax.experimental.pallas import tpu as pltpu
from jax.sharding import PartitionSpec as P

D = 768
HEADS = 12
LEN = 256


EPSILON = 1e-05
CHUNK = 32
AXES = ("fsdp", "rep")
PLACES = ("zh", "zl", "x", "c", "y")
MESH = pl.DeviceIdType.MESH


def places_and_partners():
    f = lax.axis_index("fsdp")
    r = lax.axis_index("rep")
    where = {"zh": f // 8, "zl": (f // 4) % 2, "x": (f // 2) % 2, "c": f % 2, "y": r}
    partner = {
        "zh": (f + 8 - 16 * where["zh"], r),
        "zl": (f + 4 - 8 * where["zl"], r),
        "x": (f + 2 - 4 * where["x"], r),
        "c": (f + 1 - 2 * where["c"], r),
        "y": (f, 1 - r),
    }
    return where, partner


def greet(partner):
    barrier = pltpu.get_barrier_semaphore()
    for name in PLACES:
        pl.semaphore_signal(barrier, inc=1, device_id=partner[name], device_id_type=MESH)
    pl.semaphore_wait(barrier, len(PLACES))


def gather_kernel(chunk, block_ref, all_ref, send_sem, recv_sem, own_sem):
    where, partner = places_and_partners()
    chunks = block_ref.shape[0] // chunk
    own = pltpu.make_async_copy(
        block_ref, all_ref.at[tuple(where[name] for name in PLACES)], own_sem
    )
    own.start()
    greet(partner)
    orders = (("zh", "zl", "x", "y", "c"), ("zh", "zl", "y", "x", "c"))
    copies = {}

    def begin(number, step):
        order = orders[number % 2]
        rows = pl.ds(number * chunk, chunk)
        index = tuple(
            slice(None) if name in order[:step] else where[name] for name in PLACES
        ) + (rows,)
        source = block_ref.at[rows] if step == 0 else all_ref.at[index]
        copy = pltpu.make_async_remote_copy(
            src_ref=source,
            dst_ref=all_ref.at[index],
            send_sem=send_sem.at[number, step],
            recv_sem=recv_sem.at[number, step],
            device_id=partner[order[step]],
            device_id_type=MESH,
        )
        copy.start()
        copies[number, step] = copy

    pairs = chunks // 2
    steps = len(PLACES)
    for wave in range(pairs + steps):
        for pair in range(pairs):
            step = wave - pair
            if not 0 <= step <= steps:
                continue
            for number in (2 * pair, 2 * pair + 1):
                if step == 1 and number == 0:
                    own.wait()
                if step > 0:
                    copies[number, step - 1].wait_recv()
                if step < steps:
                    begin(number, step)
    for copy in copies.values():
        copy.wait_send()


def gather_all(block, chunk):
    rows, width = block.shape
    chunks = rows // chunk
    return pl.pallas_call(
        functools.partial(gather_kernel, chunk),
        out_shape=jax.ShapeDtypeStruct((2,) * 5 + (rows, width), block.dtype),
        in_specs=[pl.BlockSpec(memory_space=pl.ANY)],
        out_specs=pl.BlockSpec(memory_space=pl.ANY),
        scratch_shapes=[
            pltpu.SemaphoreType.DMA((chunks, 5)),
            pltpu.SemaphoreType.DMA((chunks, 5)),
            pltpu.SemaphoreType.DMA,
        ],
        compiler_params=pltpu.CompilerParams(collective_id=0, has_side_effects=True),
    )(block)


def scatter_kernel(
    chunk, parts_ref, sum_ref, held, got0, got1, got2, got3, got4, send_sem, recv_sem, own_sem
):
    where, partner = places_and_partners()
    chunks = parts_ref.shape[5] // chunk
    zh, zl, x, c, y = (where[name] for name in PLACES)
    everything = slice(None)
    f32 = jnp.float32

    def rows_of(number):
        return pl.ds(number * chunk, chunk)

    own = []
    for number in range(chunks):
        rows = rows_of(number)
        copy = pltpu.make_async_copy(
            parts_ref.at[:, :, :, c, :, rows], held.at[:, :, :, :, rows], own_sem.at[number]
        )
        copy.start()
        own.append(copy)
    greet(partner)
    copies = {}

    def begin(number, step):
        rows = rows_of(number)
        x_first = number % 2 == 0
        if step == 0:
            name = "c"
            source = parts_ref.at[:, :, :, 1 - c, :, rows]
            target = got0.at[:, :, :, :, rows]
        elif step == 1:
            name = "x" if x_first else "y"
            source = held.at[:, :, 1 - x, :, rows] if x_first else held.at[:, :, :, 1 - y, rows]
            target = got1.at[:, :, :, rows]
        elif step == 2:
            name = "y" if x_first else "x"
            source = held.at[:, :, x, 1 - y, rows] if x_first else held.at[:, :, 1 - x, y, rows]
            target = got2.at[:, :, rows]
        elif step == 3:
            name = "zl"
            source = held.at[:, 1 - zl, x, y, rows]
            target = got3.at[:, rows]
        else:
            name = "zh"
            source = held.at[1 - zh, zl, x, y, rows]
            target = got4.at[rows]
        copy = pltpu.make_async_remote_copy(
            src_ref=source,
            dst_ref=target,
            send_sem=send_sem.at[number, step],
            recv_sem=recv_sem.at[number, step],
            device_id=partner[name],
            device_id_type=MESH,
        )
        copy.start()
        copies[number, step] = copy

    def add(number, step):
        rows = rows_of(number)
        x_first = number % 2 == 0
        copies[number, step].wait_recv()
        if step == 0:
            own[number].wait()

        def add_one(at, value):
            held[at] = (held[at].astype(f32) + value.astype(f32)).astype(held.dtype)

        if step == 4:
            at = (zh, zl, x, y, rows)
            sum_ref[rows] = held[at].astype(f32) + got4[rows].astype(f32)
            return

        def body(i, carry):
            if step == 0:
                four = (i // 8, (i // 4) % 2, (i // 2) % 2, i % 2)
                add_one(four + (rows,), got0[four + (rows,)])
            elif step == 1:
                three = (i // 4, (i // 2) % 2, i % 2)
                if x_first:
                    at = three[:2] + (x, three[2], rows)
                else:
                    at = three + (y, rows)
                add_one(at, got1[three + (rows,)])
            elif step == 2:
                two = (i // 2, i % 2)
                add_one(two + (x, y, rows), got2[two + (rows,)])
            else:
                add_one((i, zl, x, y, rows), got3[i, rows])
            return carry

        lax.fori_loop(0, 16 >> step, body, 0)

    for number in range(chunks):
        begin(number, 0)
    pairs = chunks // 2
    for wave in range(1, pairs + 5):
        for pair in range(pairs):
            step = wave - pair
            if not 1 <= step <= 5:
                continue
            for number in (2 * pair, 2 * pair + 1):
                add(number, step - 1)
                if step < 5:
                    begin(number, step)
    for copy in copies.values():
        copy.wait_send()


def scatter_sum(parts, chunk):
    rows, width = parts.shape[5:]
    chunks = rows // chunk
    low = parts.dtype
    return pl.pallas_call(
        functools.partial(scatter_kernel, chunk),
        out_shape=jax.ShapeDtypeStruct((rows, width), jnp.float32),
        in_specs=[pl.BlockSpec(memory_space=pl.ANY)],
        out_specs=pl.BlockSpec(memory_space=pltpu.VMEM),
        scratch_shapes=[
            pltpu.VMEM((2, 2, 2, 2, rows, width), low),
            pltpu.VMEM((2, 2, 2, 2, rows, width), low),
            pltpu.VMEM((2, 2, 2, rows, width), low),
            pltpu.VMEM((2, 2, rows, width), low),
            pltpu.VMEM((2, rows, width), low),
            pltpu.VMEM((rows, width), low),
            pltpu.SemaphoreType.DMA((chunks, 5)),
            pltpu.SemaphoreType.DMA((chunks, 5)),
            pltpu.SemaphoreType.DMA((chunks,)),
        ],
        compiler_params=pltpu.CompilerParams(
            collective_id=1, has_side_effects=True, vmem_limit_bytes=40 * 1024 * 1024
        ),
    )(parts)


def columns_to_rows(weight):
    return [weight[:, at : at + D] for at in range(0, weight.shape[1], D)]


def gather_params(params):
    ag, ash, wq, bq, bv, wo, bo, mg, ms, wu, bu, wd, bd = params
    count = D // wq.shape[0]
    if wq.shape[0] % 8 or count != 32:
        return tuple(lax.all_gather(p, AXES, axis=0, tiled=True) for p in params)
    small = jnp.concatenate([ag, ash, bq, bv, bo, mg, ms, bd, bu])
    small = jnp.pad(small, (0, D - small.shape[0]))[None]
    pieces = columns_to_rows(wq) + [wo] + columns_to_rows(wu) + [wd, small]
    used = sum(piece.shape[0] for piece in pieces)
    rows = -(-used // (2 * CHUNK)) * 2 * CHUNK
    block = jnp.pad(jnp.concatenate(pieces, axis=0), ((0, rows - used), (0, 0)))
    whole = gather_all(block, CHUNK).reshape(count, rows, D)
    n, m = wq.shape[0], wd.shape[0]
    at = 0

    def wide(parts):
        nonlocal at
        taken = [whole[:, at + n * i : at + n * (i + 1)].reshape(D, D) for i in range(parts)]
        at += n * parts
        return jnp.concatenate(taken, axis=1) if parts > 1 else taken[0]

    mat_qkv, mat_out, mat_up = wide(3), wide(1), wide(wu.shape[1] // D)
    mat_down = whole[:, at : at + m].reshape(count * m, D)
    line = whole[:, at + m]
    vectors = [line[:, n * i : n * (i + 1)].reshape(D) for i in range(8)]
    up_line = line[:, 8 * n : 8 * n + bu.shape[0]].reshape(-1)
    a, b, c, d, e, f, g, h = vectors
    return (a, b, mat_qkv, c, d, mat_out, e, f, g, mat_up, up_line, mat_down, h)


def scatter_grads(grads, n, m):
    ag, ash, wq, bq, bv, wo, bo, mg, ms, wu, bu, wd, bd = grads
    count = D // n
    if n % 8 or count != 32:
        return tuple(lax.psum_scatter(g, AXES, scatter_dimension=0, tiled=True) for g in grads)
    low16 = jnp.bfloat16
    small = jnp.concatenate(
        [v.reshape(count, n) for v in (ag, ash, bq, bv, bo, mg, ms, bd)] + [bu.reshape(count, -1)],
        axis=1,
    )
    small = jnp.pad(small, ((0, 0), (0, D - small.shape[1])))[:, None].astype(low16)
    pieces = [
        part.reshape(count, n, D)
        for weight in (wq, wo, wu)
        for part in columns_to_rows(weight.astype(low16))
    ] + [wd.astype(low16).reshape(count, m, D), small]
    used = sum(piece.shape[1] for piece in pieces)
    rows = -(-used // (2 * CHUNK)) * 2 * CHUNK
    parts = jnp.pad(jnp.concatenate(pieces, axis=1), ((0, 0), (0, rows - used), (0, 0)))
    total = scatter_sum(parts.reshape((2,) * 5 + (rows, D)), CHUNK)
    at = 0

    def wide(parts):
        nonlocal at
        taken = [total[at + n * i : at + n * (i + 1)] for i in range(parts)]
        at += n * parts
        return jnp.concatenate(taken, axis=1) if parts > 1 else taken[0]

    g_qkv, g_out, g_up = wide(3), wide(1), wide(wu.shape[1] // D)
    g_down = total[at : at + m]
    line = total[at + m]
    a, b, c, d, e, f, g, h = [line[n * i : n * (i + 1)] for i in range(8)]
    up_line = line[8 * n : 8 * n + bu.shape[0] // count]
    return (a, b, g_qkv, c, d, g_out, e, f, g, g_up, up_line, g_down, h)


def norm_rows(values, gain, shift):
    center = values - jnp.mean(values, axis=-1, keepdims=True)
    spread = jnp.mean(center * center, axis=-1, keepdims=True)
    return center * lax.rsqrt(spread + EPSILON) * gain + shift


def gelu_tanh(values):
    return (
        0.5
        * values
        * (1.0 + jnp.tanh(0.7978845608028654 * (values + 0.044715 * values * values * values)))
    )


def block_mask(seg_block):
    places = jnp.arange(seg_block.shape[1])
    causal = places[None, :] <= places[:, None]
    same_doc = seg_block[:, :, None] == seg_block[:, None, :]
    return jnp.logical_and(same_doc, causal[None])


def masked_scores(queries, key_rows, allowed, score_scale):
    raw = jnp.einsum("sqhd,skhd->shqk", queries, key_rows, preferred_element_type=jnp.float32)
    return jnp.where(allowed[:, None], raw * score_scale, -1e30)


def local(
    tokens,
    segments,
    cotangent,
    attn_gain,
    attn_shift,
    qkv_weight,
    query_bias,
    value_bias,
    out_weight,
    out_bias,
    mlp_gain,
    mlp_shift,
    up_weight,
    up_bias,
    down_weight,
    down_bias,
):
    gathered = gather_params(
        (attn_gain, attn_shift, qkv_weight, query_bias, value_bias, out_weight, out_bias,
         mlp_gain, mlp_shift, up_weight, up_bias, down_weight, down_bias)
    )
    (
        gain_attn,
        shift_attn,
        mat_qkv,
        bias_query,
        bias_value,
        mat_out,
        bias_out,
        gain_mlp,
        shift_mlp,
        mat_up,
        bias_up,
        mat_down,
        bias_down,
    ) = gathered
    f32 = jnp.float32
    low16 = jnp.bfloat16
    seq_count = segments.shape[0]
    seq_span = min(seq_count, max(1, 512 // LEN))
    block_count = seq_count // seq_span
    head_dim = D // HEADS
    score_scale = 1.0 / math.sqrt(head_dim)
    rows_in = tokens.astype(f32)
    normed16 = norm_rows(rows_in, gain_attn.astype(f32), shift_attn.astype(f32)).astype(low16)
    qkv_bias = jnp.concatenate(
        [bias_query.astype(f32), jnp.zeros((D,), f32), bias_value.astype(f32)]
    )
    qkv16 = (jnp.dot(normed16, mat_qkv, preferred_element_type=f32) + qkv_bias).astype(low16)
    heads_view = qkv16.reshape(seq_count, LEN, 3, HEADS, head_dim)
    attn_parts = []
    lse_parts = []
    for number in range(block_count):
        first_seq = number * seq_span
        current = heads_view[first_seq : first_seq + seq_span]
        allowed = block_mask(segments[first_seq : first_seq + seq_span])
        scores = masked_scores(current[:, :, 0], current[:, :, 1], allowed, score_scale)
        row_max = jnp.max(scores, axis=-1, keepdims=True)
        exponent = jnp.exp(scores - row_max)
        totals = jnp.sum(exponent, axis=-1, keepdims=True)
        probs_low = (exponent / totals).astype(low16)
        lse_parts.append(row_max + jnp.log(totals))
        mixed = jnp.einsum(
            "shqk,skhd->sqhd", probs_low, current[:, :, 2], preferred_element_type=f32
        )
        attn_parts.append(mixed.reshape(seq_span * LEN, D))
    attended16 = jnp.concatenate(attn_parts, axis=0).astype(low16)
    branch = jnp.dot(attended16, mat_out, preferred_element_type=f32) + bias_out.astype(f32)
    resid = rows_in + branch
    normed_mlp16 = norm_rows(resid, gain_mlp.astype(f32), shift_mlp.astype(f32)).astype(low16)
    hidden_pre = jnp.dot(normed_mlp16, mat_up, preferred_element_type=f32) + bias_up.astype(f32)
    hidden16 = gelu_tanh(hidden_pre).astype(low16)
    result = resid + jnp.dot(hidden16, mat_down, preferred_element_type=f32) + bias_down.astype(f32)
    out = result.astype(low16)
    grad_out = cotangent.astype(f32)
    grad_down_weight = jnp.einsum("nf,nd->fd", hidden16, cotangent, preferred_element_type=f32)
    grad_down_bias = jnp.sum(grad_out, axis=0)
    grad_hidden = jnp.einsum("nd,fd->nf", cotangent, mat_down, preferred_element_type=f32)
    unused, gelu_pull = jax.vjp(gelu_tanh, hidden_pre)
    grad_pre16 = gelu_pull(grad_hidden)[0].astype(low16)
    grad_up_weight = jnp.einsum("nd,nf->df", normed_mlp16, grad_pre16, preferred_element_type=f32)
    grad_up_bias = jnp.sum(grad_pre16.astype(f32), axis=0)
    grad_normed_mlp = jnp.einsum("nf,df->nd", grad_pre16, mat_up, preferred_element_type=f32)
    unused, second_pull = jax.vjp(norm_rows, resid, gain_mlp.astype(f32), shift_mlp.astype(f32))
    grad_resid_part, grad_mlp_gain, grad_mlp_shift = second_pull(grad_normed_mlp)
    grad_resid = grad_out + grad_resid_part
    grad_branch16 = grad_resid.astype(low16)
    grad_out_weight = jnp.einsum("ne,nd->ed", attended16, grad_branch16, preferred_element_type=f32)
    grad_out_bias = jnp.sum(grad_branch16.astype(f32), axis=0)
    grad_attended16 = jnp.einsum(
        "nd,ed->ne", grad_branch16, mat_out, preferred_element_type=f32
    ).astype(low16)
    grad_heads = grad_attended16.reshape(seq_count, LEN, HEADS, head_dim)
    grad_parts = []
    for number in range(block_count):
        first_seq = number * seq_span
        current = heads_view[first_seq : first_seq + seq_span]
        allowed = block_mask(segments[first_seq : first_seq + seq_span])
        scores = masked_scores(current[:, :, 0], current[:, :, 1], allowed, score_scale)
        probs = jnp.exp(scores - lse_parts[number])
        probs_low = probs.astype(low16)
        grad_block = grad_heads[first_seq : first_seq + seq_span]
        grad_probs = jnp.einsum(
            "sqhd,skhd->shqk", grad_block, current[:, :, 2], preferred_element_type=f32
        )
        grad_value = jnp.einsum(
            "shqk,sqhd->skhd", probs_low, grad_block, preferred_element_type=f32
        )
        inner = jnp.sum(probs * grad_probs, axis=-1, keepdims=True)
        grad_scores = (probs * (grad_probs - inner)).astype(low16)
        grad_query = (
            jnp.einsum("shqk,skhd->sqhd", grad_scores, current[:, :, 1], preferred_element_type=f32)
            * score_scale
        )
        grad_key = (
            jnp.einsum("shqk,sqhd->skhd", grad_scores, current[:, :, 0], preferred_element_type=f32)
            * score_scale
        )
        stacked = jnp.stack([grad_query, grad_key, grad_value], axis=2).reshape(
            seq_span * LEN, 3 * D
        )
        grad_parts.append(stacked.astype(low16))
    grad_qkv16 = jnp.concatenate(grad_parts, axis=0)
    grad_qkv_weight = jnp.einsum("nd,nc->dc", normed16, grad_qkv16, preferred_element_type=f32)
    bias_sums = jnp.sum(grad_qkv16.astype(f32), axis=0)
    grad_query_bias = bias_sums[:D]
    grad_value_bias = bias_sums[2 * D :]
    grad_normed = jnp.einsum("nc,dc->nd", grad_qkv16, mat_qkv, preferred_element_type=f32)
    unused, first_pull = jax.vjp(norm_rows, rows_in, gain_attn.astype(f32), shift_attn.astype(f32))
    grad_rows_part, grad_attn_gain, grad_attn_shift = first_pull(grad_normed)
    grad_tokens = grad_resid + grad_rows_part
    shares = scatter_grads(
        (grad_attn_gain, grad_attn_shift, grad_qkv_weight, grad_query_bias, grad_value_bias,
         grad_out_weight, grad_out_bias, grad_mlp_gain, grad_mlp_shift, grad_up_weight,
         grad_up_bias, grad_down_weight, grad_down_bias),
        qkv_weight.shape[0],
        down_weight.shape[0],
    )
    return (out, grad_tokens) + shares


def solution(mesh):
    in_specs = (
        P(("fsdp", "rep"), None),
        P(("fsdp", "rep"), None),
        P(("fsdp", "rep"), None),
        P(("fsdp", "rep")),
        P(("fsdp", "rep")),
        P(("fsdp", "rep"), None),
        P(("fsdp", "rep")),
        P(("fsdp", "rep")),
        P(("fsdp", "rep"), None),
        P(("fsdp", "rep")),
        P(("fsdp", "rep")),
        P(("fsdp", "rep")),
        P(("fsdp", "rep"), None),
        P(("fsdp", "rep")),
        P(("fsdp", "rep"), None),
        P(("fsdp", "rep")),
    )
    out_specs = (
        P(("fsdp", "rep"), None),
        P(("fsdp", "rep"), None),
        P(("fsdp", "rep")),
        P(("fsdp", "rep")),
        P(("fsdp", "rep"), None),
        P(("fsdp", "rep")),
        P(("fsdp", "rep")),
        P(("fsdp", "rep"), None),
        P(("fsdp", "rep")),
        P(("fsdp", "rep")),
        P(("fsdp", "rep")),
        P(("fsdp", "rep"), None),
        P(("fsdp", "rep")),
        P(("fsdp", "rep"), None),
        P(("fsdp", "rep")),
    )
    return jax.shard_map(local, mesh=mesh, in_specs=in_specs, out_specs=out_specs, check_vma=False)
```

```python
import functools
import math

import jax
import jax.numpy as jnp
from jax import lax
from jax.experimental import pallas as pl
from jax.experimental.layout import Layout, with_layout_constraint
from jax.experimental.pallas import tpu as pltpu
from jax.sharding import PartitionSpec as P

D = 768
HEADS = 12
LEN = 256


EPSILON = 1e-05
CHUNK = 32
LANES = 128


def dot32(left, right, left_dim, right_dim):
    return lax.dot_general(
        left, right, (((left_dim,), (right_dim,)), ((), ())), preferred_element_type=jnp.float32
    )


def mask_bias(seg_rows, seg_columns):
    row = lax.broadcasted_iota(jnp.int32, (LEN, LEN), 0)
    column = lax.broadcasted_iota(jnp.int32, (LEN, LEN), 1)
    allowed = jnp.logical_and(seg_rows == seg_columns, column <= row)
    return jnp.where(allowed, 0.0, -1e30).astype(jnp.float32)


def one_head(values, first):
    lane = lax.broadcasted_iota(jnp.int32, values.shape, 1)
    return jnp.where((lane < LANES // 2) == first, values, jnp.zeros_like(values))


def softmax_rows(queries, key_rows, bias):
    scores = dot32(queries, key_rows, 1, 1) * (1.0 / math.sqrt(D // HEADS)) + bias
    exponent = jnp.exp(scores - jnp.max(scores, axis=-1, keepdims=True))
    return exponent * (1.0 / jnp.sum(exponent, axis=-1, keepdims=True))


def attend_kernel(row_ref, column_ref, qkv_ref, out_ref, bias):
    bias[...] = mask_bias(row_ref[0], column_ref[0])
    for at in range(0, D, LANES):
        queries = qkv_ref[:, at : at + LANES]
        key_rows = qkv_ref[:, D + at : D + at + LANES]
        value_rows = qkv_ref[:, 2 * D + at : 2 * D + at + LANES]
        total = None
        for first in (True, False):
            probs = softmax_rows(one_head(queries, first), key_rows, bias[...])
            mixed = dot32(probs.astype(jnp.bfloat16), one_head(value_rows, first), 1, 0)
            total = mixed if total is None else total + mixed
        out_ref[:, at : at + LANES] = total.astype(jnp.bfloat16)


def attend_back_kernel(row_ref, column_ref, qkv_ref, grad_ref, out_ref, bias):
    bias[...] = mask_bias(row_ref[0], column_ref[0])
    low16 = jnp.bfloat16
    scale = 1.0 / math.sqrt(D // HEADS)
    for at in range(0, D, LANES):
        queries = qkv_ref[:, at : at + LANES]
        key_rows = qkv_ref[:, D + at : D + at + LANES]
        value_rows = qkv_ref[:, 2 * D + at : 2 * D + at + LANES]
        grad = grad_ref[:, at : at + LANES]
        totals = None
        for first in (True, False):
            query_one = one_head(queries, first)
            grad_one = one_head(grad, first)
            probs = softmax_rows(query_one, key_rows, bias[...])
            grad_probs = dot32(grad_one, value_rows, 1, 1)
            inner = jnp.sum(probs * grad_probs, axis=-1, keepdims=True)
            grad_scores = (probs * (grad_probs - inner)).astype(low16)
            parts = (
                dot32(grad_scores, one_head(key_rows, first), 1, 0),
                dot32(grad_scores, query_one, 0, 0),
                dot32(probs.astype(low16), grad_one, 0, 0),
            )
            totals = parts if totals is None else tuple(a + b for a, b in zip(totals, parts))
        out_ref[:, at : at + LANES] = (totals[0] * scale).astype(low16)
        out_ref[:, D + at : D + at + LANES] = (totals[1] * scale).astype(low16)
        out_ref[:, 2 * D + at : 2 * D + at + LANES] = totals[2].astype(low16)


def per_sequence(kernel, segments, arrays, width):
    count = segments.shape[0]

    def whole(columns):
        return pl.BlockSpec((LEN, columns), lambda i: (i, 0))

    return pl.pallas_call(
        kernel,
        grid=(count,),
        out_shape=jax.ShapeDtypeStruct((count * LEN, width), jnp.bfloat16),
        in_specs=[
            pl.BlockSpec((1, LEN, 1), lambda i: (i, 0, 0)),
            pl.BlockSpec((1, 1, LEN), lambda i: (i, 0, 0)),
        ]
        + [whole(array.shape[1]) for array in arrays],
        out_specs=whole(width),
        scratch_shapes=[pltpu.VMEM((LEN, LEN), jnp.float32)],
        compiler_params=pltpu.CompilerParams(vmem_limit_bytes=32 * 1024 * 1024),
    )(segments[:, :, None], segments[:, None, :], *arrays)


AXES = ("fsdp", "rep")
PLACES = ("zh", "zl", "x", "c", "y")
MESH = pl.DeviceIdType.MESH


def places_and_partners():
    f = lax.axis_index("fsdp")
    r = lax.axis_index("rep")
    where = {"zh": f // 8, "zl": (f // 4) % 2, "x": (f // 2) % 2, "c": f % 2, "y": r}
    partner = {
        "zh": (f + 8 - 16 * where["zh"], r),
        "zl": (f + 4 - 8 * where["zl"], r),
        "x": (f + 2 - 4 * where["x"], r),
        "c": (f + 1 - 2 * where["c"], r),
        "y": (f, 1 - r),
    }
    return where, partner


def greet(partner):
    barrier = pltpu.get_barrier_semaphore()
    for name in PLACES:
        pl.semaphore_signal(barrier, inc=1, device_id=partner[name], device_id_type=MESH)
    pl.semaphore_wait(barrier, len(PLACES))


def gather_kernel(chunk, block_ref, all_ref, send_sem, recv_sem, own_sem):
    where, partner = places_and_partners()
    total_rows = block_ref.shape[0]
    chunks = -(-total_rows // chunk)
    own = pltpu.make_async_copy(
        block_ref, all_ref.at[tuple(where[name] for name in PLACES)], own_sem
    )
    own.start()
    greet(partner)
    orders = (("zh", "zl", "x", "y", "c"), ("zh", "zl", "y", "x", "c"))
    copies = {}

    def begin(number, step):
        order = orders[number % 2]
        rows = pl.ds(number * chunk, min(chunk, total_rows - number * chunk))
        index = tuple(
            slice(None) if name in order[:step] else where[name] for name in PLACES
        ) + (rows,)
        source = block_ref.at[rows] if step == 0 else all_ref.at[index]
        copy = pltpu.make_async_remote_copy(
            src_ref=source,
            dst_ref=all_ref.at[index],
            send_sem=send_sem.at[number, step],
            recv_sem=recv_sem.at[number, step],
            device_id=partner[order[step]],
            device_id_type=MESH,
        )
        copy.start()
        copies[number, step] = copy

    pairs = -(-chunks // 2)
    steps = len(PLACES)
    for wave in range(pairs + steps):
        for pair in range(pairs):
            step = wave - pair
            if not 0 <= step <= steps:
                continue
            for number in range(2 * pair, min(2 * pair + 2, chunks)):
                if step == 1 and number == 0:
                    own.wait()
                if step > 0:
                    copies[number, step - 1].wait_recv()
                if step < steps:
                    begin(number, step)
    for copy in copies.values():
        copy.wait_send()


def gather_all(block, chunk):
    rows, width = block.shape
    chunks = -(-rows // chunk)
    return pl.pallas_call(
        functools.partial(gather_kernel, chunk),
        out_shape=jax.ShapeDtypeStruct((2,) * 5 + (rows, width), block.dtype),
        in_specs=[pl.BlockSpec(memory_space=pl.ANY)],
        out_specs=pl.BlockSpec(memory_space=pl.ANY),
        scratch_shapes=[
            pltpu.SemaphoreType.DMA((chunks, 5)),
            pltpu.SemaphoreType.DMA((chunks, 5)),
            pltpu.SemaphoreType.DMA,
        ],
        compiler_params=pltpu.CompilerParams(collective_id=0, has_side_effects=True),
    )(block)


def scatter_kernel(
    chunk, parts_ref, sum_ref, held, got0, got1, got2, got3, got4, send_sem, recv_sem, own_sem
):
    where, partner = places_and_partners()
    total_rows = parts_ref.shape[5]
    chunks = -(-total_rows // chunk)
    zh, zl, x, c, y = (where[name] for name in PLACES)
    everything = slice(None)
    f32 = jnp.float32

    def rows_of(number):
        return pl.ds(number * chunk, min(chunk, total_rows - number * chunk))

    own = []
    for number in range(chunks):
        rows = rows_of(number)
        copy = pltpu.make_async_copy(
            parts_ref.at[:, :, :, c, :, rows], held.at[:, :, :, :, rows], own_sem.at[number]
        )
        copy.start()
        own.append(copy)
    greet(partner)
    copies = {}

    def begin(number, step):
        rows = rows_of(number)
        x_first = number % 2 == 0
        if step == 0:
            name = "c"
            source = parts_ref.at[:, :, :, 1 - c, :, rows]
            target = got0.at[:, :, :, :, rows]
        elif step == 1:
            name = "x" if x_first else "y"
            source = held.at[:, :, 1 - x, :, rows] if x_first else held.at[:, :, :, 1 - y, rows]
            target = got1.at[:, :, :, rows]
        elif step == 2:
            name = "y" if x_first else "x"
            source = held.at[:, :, x, 1 - y, rows] if x_first else held.at[:, :, 1 - x, y, rows]
            target = got2.at[:, :, rows]
        elif step == 3:
            name = "zl"
            source = held.at[:, 1 - zl, x, y, rows]
            target = got3.at[:, rows]
        else:
            name = "zh"
            source = held.at[1 - zh, zl, x, y, rows]
            target = got4.at[rows]
        copy = pltpu.make_async_remote_copy(
            src_ref=source,
            dst_ref=target,
            send_sem=send_sem.at[number, step],
            recv_sem=recv_sem.at[number, step],
            device_id=partner[name],
            device_id_type=MESH,
        )
        copy.start()
        copies[number, step] = copy

    def add(number, step):
        rows = rows_of(number)
        x_first = number % 2 == 0
        copies[number, step].wait_recv()
        if step == 0:
            own[number].wait()

        def add_one(at, value):
            held[at] = (held[at].astype(f32) + value.astype(f32)).astype(held.dtype)

        if step == 4:
            at = (zh, zl, x, y, rows)
            sum_ref[rows] = held[at].astype(f32) + got4[rows].astype(f32)
            return

        def body(i, carry):
            if step == 0:
                four = (i // 8, (i // 4) % 2, (i // 2) % 2, i % 2)
                add_one(four + (rows,), got0[four + (rows,)])
            elif step == 1:
                three = (i // 4, (i // 2) % 2, i % 2)
                if x_first:
                    at = three[:2] + (x, three[2], rows)
                else:
                    at = three + (y, rows)
                add_one(at, got1[three + (rows,)])
            elif step == 2:
                two = (i // 2, i % 2)
                add_one(two + (x, y, rows), got2[two + (rows,)])
            else:
                add_one((i, zl, x, y, rows), got3[i, rows])
            return carry

        lax.fori_loop(0, 16 >> step, body, 0)

    for number in range(chunks):
        begin(number, 0)
    pairs = -(-chunks // 2)
    for wave in range(1, pairs + 5):
        for pair in range(pairs):
            step = wave - pair
            if not 1 <= step <= 5:
                continue
            for number in range(2 * pair, min(2 * pair + 2, chunks)):
                add(number, step - 1)
                if step < 5:
                    begin(number, step)
    for copy in copies.values():
        copy.wait_send()


def scatter_sum(parts, chunk):
    rows, width = parts.shape[5:]
    chunks = -(-rows // chunk)
    low = parts.dtype
    return pl.pallas_call(
        functools.partial(scatter_kernel, chunk),
        out_shape=jax.ShapeDtypeStruct((rows, width), jnp.float32),
        in_specs=[pl.BlockSpec(memory_space=pl.ANY)],
        out_specs=pl.BlockSpec(memory_space=pltpu.VMEM),
        scratch_shapes=[
            pltpu.VMEM((2, 2, 2, 2, rows, width), low),
            pltpu.VMEM((2, 2, 2, 2, rows, width), low),
            pltpu.VMEM((2, 2, 2, rows, width), low),
            pltpu.VMEM((2, 2, rows, width), low),
            pltpu.VMEM((2, rows, width), low),
            pltpu.VMEM((rows, width), low),
            pltpu.SemaphoreType.DMA((chunks, 5)),
            pltpu.SemaphoreType.DMA((chunks, 5)),
            pltpu.SemaphoreType.DMA((chunks,)),
        ],
        compiler_params=pltpu.CompilerParams(
            collective_id=1, has_side_effects=True, vmem_limit_bytes=40 * 1024 * 1024
        ),
    )(parts)


def columns_to_rows(weight):
    return [weight[:, at : at + D] for at in range(0, weight.shape[1], D)]


def gather_params(params):
    ag, ash, wq, bq, bv, wo, bo, mg, ms, wu, bu, wd, bd = params
    count = D // wq.shape[0]
    if wq.shape[0] % 8 or count != 32:
        return tuple(lax.all_gather(p, AXES, axis=0, tiled=True) for p in params)
    small = jnp.concatenate([ag, ash, bq, bv, bo, mg, ms, bd, bu])
    small = jnp.pad(small, (0, D - small.shape[0]))[None]
    pieces = columns_to_rows(wq) + [wo] + columns_to_rows(wu) + [wd, small]
    used = sum(piece.shape[0] for piece in pieces)
    rows = -(-used // 16) * 16
    block = jnp.pad(jnp.concatenate(pieces, axis=0), ((0, rows - used), (0, 0)))
    whole = gather_all(block, CHUNK).reshape(count, rows, D)
    n, m = wq.shape[0], wd.shape[0]
    at = 0

    def wide(parts):
        nonlocal at
        taken = [whole[:, at + n * i : at + n * (i + 1)].reshape(D, D) for i in range(parts)]
        at += n * parts
        return jnp.concatenate(taken, axis=1) if parts > 1 else taken[0]

    mat_qkv, mat_out, mat_up = wide(3), wide(1), wide(wu.shape[1] // D)
    mat_down = whole[:, at : at + m].reshape(count * m, D)
    line = whole[:, at + m]
    vectors = [line[:, n * i : n * (i + 1)].reshape(D) for i in range(8)]
    up_line = line[:, 8 * n : 8 * n + bu.shape[0]].reshape(-1)
    a, b, c, d, e, f, g, h = vectors
    return (a, b, mat_qkv, c, d, mat_out, e, f, g, mat_up, up_line, mat_down, h)


def scatter_grads(grads, n, m):
    ag, ash, wq, bq, bv, wo, bo, mg, ms, wu, bu, wd, bd = grads
    count = D // n
    if n % 8 or count != 32:
        return tuple(lax.psum_scatter(g, AXES, scatter_dimension=0, tiled=True) for g in grads)
    low16 = jnp.bfloat16
    small = jnp.concatenate(
        [v.reshape(count, n) for v in (ag, ash, bq, bv, bo, mg, ms, bd)] + [bu.reshape(count, -1)],
        axis=1,
    )
    small = jnp.pad(small, ((0, 0), (0, D - small.shape[1])))[:, None].astype(low16)
    pieces = [
        part.reshape(count, n, D)
        for weight in (wq, wo, wu)
        for part in columns_to_rows(weight.astype(low16))
    ] + [wd.astype(low16).reshape(count, m, D), small]
    used = sum(piece.shape[1] for piece in pieces)
    rows = -(-used // 16) * 16
    parts = jnp.pad(jnp.concatenate(pieces, axis=1), ((0, 0), (0, rows - used), (0, 0)))
    total = scatter_sum(parts.reshape((2,) * 5 + (rows, D)), CHUNK)
    at = 0

    def wide(parts):
        nonlocal at
        taken = [total[at + n * i : at + n * (i + 1)] for i in range(parts)]
        at += n * parts
        return jnp.concatenate(taken, axis=1) if parts > 1 else taken[0]

    g_qkv, g_out, g_up = wide(3), wide(1), wide(wu.shape[1] // D)
    g_down = total[at : at + m]
    line = total[at + m]
    a, b, c, d, e, f, g, h = [line[n * i : n * (i + 1)] for i in range(8)]
    up_line = line[8 * n : 8 * n + bu.shape[0] // count]
    return (a, b, g_qkv, c, d, g_out, e, f, g, g_up, up_line, g_down, h)


def norm_rows(values, gain, shift):
    center = values - jnp.mean(values, axis=-1, keepdims=True)
    spread = jnp.mean(center * center, axis=-1, keepdims=True)
    return center * lax.rsqrt(spread + EPSILON) * gain + shift


def gelu_tanh(values):
    return (
        0.5
        * values
        * (1.0 + jnp.tanh(0.7978845608028654 * (values + 0.044715 * values * values * values)))
    )


def by_rows(values):
    return with_layout_constraint(values, Layout(major_to_minor=(0, 1)))


def local(
    tokens,
    segments,
    cotangent,
    attn_gain,
    attn_shift,
    qkv_weight,
    query_bias,
    value_bias,
    out_weight,
    out_bias,
    mlp_gain,
    mlp_shift,
    up_weight,
    up_bias,
    down_weight,
    down_bias,
):
    gathered = gather_params(
        (attn_gain, attn_shift, qkv_weight, query_bias, value_bias, out_weight, out_bias,
         mlp_gain, mlp_shift, up_weight, up_bias, down_weight, down_bias)
    )
    (
        gain_attn,
        shift_attn,
        mat_qkv,
        bias_query,
        bias_value,
        mat_out,
        bias_out,
        gain_mlp,
        shift_mlp,
        mat_up,
        bias_up,
        mat_down,
        bias_down,
    ) = gathered
    f32 = jnp.float32
    low16 = jnp.bfloat16
    rows_in = tokens.astype(f32)
    normed16 = norm_rows(rows_in, gain_attn.astype(f32), shift_attn.astype(f32)).astype(low16)
    qkv_bias = jnp.concatenate(
        [bias_query.astype(f32), jnp.zeros((D,), f32), bias_value.astype(f32)]
    )
    qkv16 = (jnp.dot(normed16, mat_qkv, preferred_element_type=f32) + qkv_bias).astype(low16)
    attended16 = per_sequence(attend_kernel, segments, (qkv16,), D)
    branch = jnp.dot(attended16, mat_out, preferred_element_type=f32) + bias_out.astype(f32)
    resid = by_rows(rows_in + branch)
    normed_mlp16 = norm_rows(resid, gain_mlp.astype(f32), shift_mlp.astype(f32)).astype(low16)
    hidden_pre = jnp.dot(normed_mlp16, mat_up, preferred_element_type=f32) + bias_up.astype(f32)
    hidden16 = gelu_tanh(hidden_pre).astype(low16)
    result = resid + jnp.dot(hidden16, mat_down, preferred_element_type=f32) + bias_down.astype(f32)
    out = result.astype(low16)
    grad_out = cotangent.astype(f32)
    grad_down_weight = jnp.einsum("nf,nd->fd", hidden16, cotangent, preferred_element_type=f32)
    grad_down_bias = jnp.sum(grad_out, axis=0)
    grad_hidden = jnp.einsum("nd,fd->nf", cotangent, mat_down, preferred_element_type=f32)
    unused, gelu_pull = jax.vjp(gelu_tanh, hidden_pre)
    grad_pre16 = gelu_pull(grad_hidden)[0].astype(low16)
    grad_up_weight = jnp.einsum("nd,nf->df", normed_mlp16, grad_pre16, preferred_element_type=f32)
    grad_up_bias = jnp.sum(grad_pre16.astype(f32), axis=0)
    grad_normed_mlp = by_rows(jnp.einsum("nf,df->nd", grad_pre16, mat_up, preferred_element_type=f32))
    unused, second_pull = jax.vjp(norm_rows, resid, gain_mlp.astype(f32), shift_mlp.astype(f32))
    grad_resid_part, grad_mlp_gain, grad_mlp_shift = second_pull(grad_normed_mlp)
    grad_resid = by_rows(grad_out + grad_resid_part)
    grad_branch16 = grad_resid.astype(low16)
    grad_out_weight = jnp.einsum("ne,nd->ed", attended16, grad_branch16, preferred_element_type=f32)
    grad_out_bias = jnp.sum(grad_branch16.astype(f32), axis=0)
    grad_attended16 = jnp.einsum(
        "nd,ed->ne", grad_branch16, mat_out, preferred_element_type=f32
    ).astype(low16)
    grad_qkv16 = per_sequence(attend_back_kernel, segments, (qkv16, grad_attended16), 3 * D)
    grad_qkv_weight = jnp.einsum("nd,nc->dc", normed16, grad_qkv16, preferred_element_type=f32)
    bias_sums = jnp.sum(grad_qkv16.astype(f32), axis=0)
    grad_query_bias = bias_sums[:D]
    grad_value_bias = bias_sums[2 * D :]
    grad_normed = by_rows(jnp.einsum("nc,dc->nd", grad_qkv16, mat_qkv, preferred_element_type=f32))
    unused, first_pull = jax.vjp(norm_rows, rows_in, gain_attn.astype(f32), shift_attn.astype(f32))
    grad_rows_part, grad_attn_gain, grad_attn_shift = first_pull(grad_normed)
    grad_tokens = grad_resid + grad_rows_part
    shares = scatter_grads(
        (grad_attn_gain, grad_attn_shift, grad_qkv_weight, grad_query_bias, grad_value_bias,
         grad_out_weight, grad_out_bias, grad_mlp_gain, grad_mlp_shift, grad_up_weight,
         grad_up_bias, grad_down_weight, grad_down_bias),
        qkv_weight.shape[0],
        down_weight.shape[0],
    )
    return (out, grad_tokens) + shares


def solution(mesh):
    in_specs = (
        P(("fsdp", "rep"), None),
        P(("fsdp", "rep"), None),
        P(("fsdp", "rep"), None),
        P(("fsdp", "rep")),
        P(("fsdp", "rep")),
        P(("fsdp", "rep"), None),
        P(("fsdp", "rep")),
        P(("fsdp", "rep")),
        P(("fsdp", "rep"), None),
        P(("fsdp", "rep")),
        P(("fsdp", "rep")),
        P(("fsdp", "rep")),
        P(("fsdp", "rep"), None),
        P(("fsdp", "rep")),
        P(("fsdp", "rep"), None),
        P(("fsdp", "rep")),
    )
    out_specs = (
        P(("fsdp", "rep"), None),
        P(("fsdp", "rep"), None),
        P(("fsdp", "rep")),
        P(("fsdp", "rep")),
        P(("fsdp", "rep"), None),
        P(("fsdp", "rep")),
        P(("fsdp", "rep")),
        P(("fsdp", "rep"), None),
        P(("fsdp", "rep")),
        P(("fsdp", "rep")),
        P(("fsdp", "rep")),
        P(("fsdp", "rep"), None),
        P(("fsdp", "rep")),
        P(("fsdp", "rep"), None),
        P(("fsdp", "rep")),
    )
    return jax.shard_map(local, mesh=mesh, in_specs=in_specs, out_specs=out_specs, check_vma=False)
```
